128 devices in a mesh: tok: 8 (over z, core), exp: 16 (over x, y).
Axes of the slice: x: 4, y: 4, z: 4, core: 2. Of those that a mesh axis runs over, the one named last changes fastest.
Arguments:
- tokens: bfloat16 [8192, 4096], P('tok', 'exp'), may hold values from -6 to 6
- cotangent: bfloat16 [8192, 4096], P('tok', 'exp'), may hold values from -1.5 to 1.5
- gates: float32 [8192, 16], P('tok'), may hold values from 0.05 to 1
- picks: int32 [8, 16], replicated, may hold values from 0 to 8, as said below
- w_in: bfloat16 [16, 4096, 8192], P('exp', None, 'tok'), may hold values from -0.09375 to 0.09375
- w_out: bfloat16 [16, 8192, 4096], P('exp', 'tok'), may hold values from -0.0625 to 0.0625
Outputs:
- mixed: bfloat16 [8192, 4096], P('tok', 'exp')
- d_tokens: bfloat16 [8192, 4096], P('tok', 'exp')
- d_gates: float32 [8192, 16], P('tok')
The draws below stay inside these ranges and needn't reach their ends.
Inputs may be any that keep to these rules, and one draw needn't show every extreme that they name: `picks`: each column has exactly 6 entries below 8; the value 8 means that the expert takes no block of that tile.
All inputs are finite; a program needn't handle non-finite values.
Results may differ from the reference program's by a relative error of at most 0.0069.
Values may be sent and summed in bfloat16 or wider, within the bound.
No kernel may reach another device: no remote copies, remote signals or barrier semaphores. Data moves between devices by JAX's collectives and lax.ppermute only.
A program may use at most 128 MiB of HBM per device.

```python
import math
import jax
import jax.numpy as jnp
from jax import lax

D = 4096
FFW = 8192
BLK = 128
TILE_BLK = 8
TILES = 8
EXPERTS = 16
CAP = 6
TOKENS = 8192


def draw_picks(key, part):
    key = jax.random.fold_in(key, 7)
    score_key, block_key = jax.random.split(key)
    raw_scores = jax.random.randint(score_key, (TILES, EXPERTS), 0, 1048576)
    tile_ids = jnp.arange(TILES, dtype=jnp.int32)[:, None]
    scores = raw_scores * TILES + tile_ids
    ordering = jnp.argsort(scores, axis=0)
    ranking = jnp.argsort(ordering, axis=0)
    chosen = ranking < CAP
    block_pick = jax.random.randint(block_key, (TILES, EXPERTS), 0, TILE_BLK)
    return jnp.where(chosen, block_pick, TILE_BLK).astype(jnp.int32)


def shard_levels(stream_key, dims, shards, least, high):
    gain, own = 1.0, jax.random.fold_in(stream_key, 6)
    for dim, parts in shards:
        heights = jnp.exp(jax.random.uniform(jax.random.fold_in(own, dim), (parts,), jnp.float32, least / len(shards), high / len(shards)))
        gain = gain * jnp.repeat(heights, dims[dim] // parts).reshape([-1 if axis == dim else 1 for axis in range(len(dims))])
    return gain


def scatter_about(stream_key, shape, width, limit, cuts=(), held_as=jnp.bfloat16):
    result = width * jax.random.normal(stream_key, shape, jnp.float32)
    if cuts:
        result = result * shard_levels(stream_key, shape, cuts, -0.22, 0.18)
    return jnp.clip(result, -limit, limit).astype(held_as)


def setup_inputs(seed: int = 0) -> dict:
    seeds = jax.random.split(jax.random.key(seed), 7)
    tokens = scatter_about(seeds[0], (TOKENS, D), 1.0, 6.0, ((0, 8), (1, 16)))
    cotangent = scatter_about(seeds[1], (TOKENS, D), 0.25, 1.5, ((0, 8), (1, 16)))
    gates = jnp.clip(jnp.exp(math.log(1.0) - 2.9957323 * jax.random.uniform(seeds[2], (TOKENS, EXPERTS), jnp.float32) ** shard_levels(seeds[2], (TOKENS, EXPERTS), ((0, 8),), -0.2, 0.2)), 0.05, 1.0)
    picks = draw_picks(jax.random.fold_in(seeds[6], 71), 0)
    w_in = scatter_about(seeds[4], (EXPERTS, D, FFW), D ** -0.5, 0.09375, ((0, 16), (2, 8)))
    w_out = scatter_about(seeds[5], (EXPERTS, FFW, D), FFW ** -0.5, 0.0625, ((0, 16), (1, 8)))
    return {"tokens": tokens, "cotangent": cotangent, "gates": gates, "picks": picks, "w_in": w_in, "w_out": w_out}


def gelu_tanh(value):
    return jax.nn.gelu(value, approximate=True)

def round_trip(value):
    return lax.optimization_barrier(value.astype(jnp.bfloat16)).astype(jnp.float32)

def reference(tokens, cotangent, gates, picks, w_in, w_out):
    tiles = picks.shape[0]
    experts = picks.shape[1]
    feature_count = tokens.shape[1]
    blocks = tokens.shape[0] // (tiles * BLK)
    slice_units = w_in.shape[2] // tiles
    tok_four = tokens.astype(jnp.float32).reshape(tiles, blocks, BLK, feature_count)
    cot_four = cotangent.astype(jnp.float32).reshape(tiles, blocks, BLK, feature_count)
    gate_four = gates.reshape(tiles, blocks, BLK, experts)
    mixed = jnp.zeros((tiles, blocks, BLK, feature_count), jnp.float32)
    d_tokens = jnp.zeros((tiles, blocks, BLK, feature_count), jnp.float32)
    d_gates = jnp.zeros((tiles, blocks, BLK, experts), jnp.float32)
    block_ids = jnp.arange(blocks, dtype=jnp.int32)
    for expert in range(experts):
        selector = (picks[:, expert][:, None] == block_ids[None, :]).astype(jnp.float32)
        x_rows = jnp.einsum('tb,tbrc->trc', selector, tok_four, precision=lax.Precision.HIGHEST)
        dy_rows = jnp.einsum('tb,tbrc->trc', selector, cot_four, precision=lax.Precision.HIGHEST)
        gate_rows = jnp.einsum('tb,tbr->tr', selector, gate_four[..., expert], precision=lax.Precision.HIGHEST)
        x_flat = x_rows.astype(jnp.bfloat16).reshape(tiles * BLK, feature_count)
        g_flat = (gate_rows[..., None] * dy_rows).astype(jnp.bfloat16).reshape(tiles * BLK, feature_count)
        hidden = jnp.dot(x_flat, w_in[expert], preferred_element_type=jnp.float32)
        act, gelu_back = jax.vjp(gelu_tanh, hidden)
        act_low = act.astype(jnp.bfloat16)
        act_grad = lax.dot_general(g_flat, w_out[expert], (((1,), (1,)), ((), ())), preferred_element_type=jnp.float32)
        hidden_grad = gelu_back(act_grad)[0].astype(jnp.bfloat16)
        out_sum = jnp.zeros((tiles * BLK, feature_count), jnp.float32)
        grad_sum = jnp.zeros((tiles * BLK, feature_count), jnp.float32)
        for part_index in range(tiles):
            low = part_index * slice_units
            high = low + slice_units
            out_term = jnp.dot(act_low[:, low:high], w_out[expert, low:high, :], preferred_element_type=jnp.float32)
            grad_term = lax.dot_general(hidden_grad[:, low:high], w_in[expert, :, low:high], (((1,), (1,)), ((), ())), preferred_element_type=jnp.float32)
            out_sum = out_sum + round_trip(out_term)
            grad_sum = grad_sum + round_trip(grad_term)
        out_rows = round_trip(out_sum).reshape(tiles, BLK, feature_count)
        grad_rows = round_trip(grad_sum).reshape(tiles, BLK, feature_count)
        mask_four = selector[:, :, None, None]
        mixed = mixed + mask_four * (gate_rows[..., None] * out_rows)[:, None]
        d_tokens = d_tokens + mask_four * grad_rows[:, None]
        gate_term = lax.optimization_barrier(jnp.sum(dy_rows * out_rows, axis=-1))
        d_gates = d_gates.at[..., expert].add(selector[:, :, None] * gate_term[:, None])
    total = tiles * blocks * BLK
    return (mixed.reshape(total, feature_count).astype(jnp.bfloat16), d_tokens.reshape(total, feature_count).astype(jnp.bfloat16), d_gates.reshape(total, experts))
```

```python
import functools

import jax
import jax.numpy as jnp
from jax import lax
from jax.experimental import pallas as pl
from jax.experimental.pallas import tpu as pltpu
from jax.sharding import PartitionSpec as P

D = 4096
BLK = 128
WIDTH = 256
SLICES = D // WIDTH
CAP = 6
OWN = CAP // 2
ROWS = OWN * BLK
UNITS = 1024
GELU_C = 0.7978845608028654
GELU_K = 0.044715
MIB = 1024 * 1024
ANY = pl.BlockSpec(memory_space=pl.ANY)
SMEM = pl.BlockSpec(memory_space=pltpu.SMEM)
VMEM = pl.BlockSpec(memory_space=pltpu.VMEM)


def params(mib=56):
    return pltpu.CompilerParams(vmem_limit_bytes=mib * MIB)


def cost(flops, nbytes):
    return pl.CostEstimate(flops=flops, bytes_accessed=nbytes, transcendentals=0)


def pick_body(count, ids, src, out, sems):
    copies = [
        pltpu.make_async_copy(src.at[ids[i]], out.at[i], sems.at[i]) for i in range(count)
    ]
    for copy in copies:
        copy.start()
    for copy in copies:
        copy.wait()


def pick_blocks(src, ids):
    count = ids.shape[0]
    return pl.pallas_call(
        functools.partial(pick_body, count),
        out_shape=jax.ShapeDtypeStruct((count, BLK, WIDTH), src.dtype),
        in_specs=[SMEM, ANY],
        out_specs=ANY,
        scratch_shapes=[pltpu.SemaphoreType.DMA((count,))],
        cost_estimate=cost(0, 2 * count * BLK * WIDTH * 2),
        name="pick_blocks",
    )(ids, src)


def hidden_body(tiles, x_all, wa, wb, act_a, act_b, der_a, der_b, x_v, sems):
    @pl.when(pl.program_id(0) == 0)
    def _():
        copies = [
            pltpu.make_async_copy(
                x_all.at[tiles[s], f],
                x_v.at[pl.ds(s * BLK, BLK), pl.ds(f * WIDTH, WIDTH)],
                sems.at[s, f],
            )
            for s in range(OWN)
            for f in range(SLICES)
        ]
        for copy in copies:
            copy.start()
        for copy in copies:
            copy.wait()

    for w, act, der in ((wa, act_a, der_a), (wb, act_b, der_b)):
        h = jnp.dot(x_v[...], w[...], preferred_element_type=jnp.float32)
        sq = h * h
        t = jnp.tanh(GELU_C * h * (1.0 + GELU_K * sq))
        half = 0.5 * (1.0 + t)
        act[...] = (h * half).astype(act.dtype)
        der[...] = half + (0.5 * GELU_C) * h * (1.0 - t * t) * (1.0 + (3.0 * GELU_K) * sq)


def hidden(tiles, x_all, w_in, w_in_other):
    cols = 256
    w_spec = pl.BlockSpec((D, cols), lambda i: (0, i))
    o_spec = pl.BlockSpec((ROWS, cols), lambda i: (0, i))
    act = jax.ShapeDtypeStruct((ROWS, UNITS), jnp.bfloat16)
    der = jax.ShapeDtypeStruct((ROWS, UNITS), jnp.float32)
    return pl.pallas_call(
        hidden_body,
        grid=(UNITS // cols,),
        out_shape=(act, act, der, der),
        in_specs=[SMEM, ANY, w_spec, w_spec],
        out_specs=(o_spec, o_spec, o_spec, o_spec),
        scratch_shapes=[
            pltpu.VMEM((ROWS, D), jnp.bfloat16),
            pltpu.SemaphoreType.DMA((OWN, SLICES)),
        ],
        compiler_params=params(),
        cost_estimate=cost(2 * ROWS * D * 2 * UNITS, 24 * MIB),
        name="hidden",
    )(tiles, x_all, w_in, w_in_other)


def back_body(dy, wa, wb, act_a, act_b, der_a, der_b, gate, dh_a, dh_b, dgate, dy_v, sems):
    step = pl.program_id(0)

    @pl.when(step == 0)
    def _():
        copies = [
            pltpu.make_async_copy(dy.at[f], dy_v.at[:, pl.ds(f * WIDTH, WIDTH)], sems.at[f])
            for f in range(SLICES)
        ]
        for copy in copies:
            copy.start()
        for copy in copies:
            copy.wait()
        dgate[...] = jnp.zeros_like(dgate)

    scale = gate[...]
    total = dgate[...]
    for w, act, der, dh in ((wa, act_a, der_a, dh_a), (wb, act_b, der_b, dh_b)):
        u = lax.dot_general(
            dy_v[...], w[...], (((1,), (1,)), ((), ())), preferred_element_type=jnp.float32
        )
        dh[...] = (scale * u * der[...]).astype(dh.dtype)
        total += jnp.sum(act[...].astype(jnp.float32) * u, axis=1, keepdims=True)
    dgate[...] = total


def back(dy, w_out, w_out_other, acts, ders, gate):
    cols = 256
    w_spec = pl.BlockSpec((cols, D), lambda i: (i, 0))
    o_spec = pl.BlockSpec((ROWS, cols), lambda i: (0, i))
    g_spec = pl.BlockSpec((ROWS, 1), lambda i: (0, 0))
    dh = jax.ShapeDtypeStruct((ROWS, UNITS), jnp.bfloat16)
    return pl.pallas_call(
        back_body,
        grid=(UNITS // cols,),
        out_shape=(dh, dh, jax.ShapeDtypeStruct((ROWS, 1), jnp.float32)),
        in_specs=[ANY, w_spec, w_spec, o_spec, o_spec, o_spec, o_spec, g_spec],
        out_specs=(o_spec, o_spec, g_spec),
        scratch_shapes=[
            pltpu.VMEM((ROWS, D), jnp.bfloat16),
            pltpu.SemaphoreType.DMA((SLICES,)),
        ],
        compiler_params=params(),
        cost_estimate=cost(2 * ROWS * D * 2 * UNITS, 24 * MIB),
        name="back",
    )(dy, w_out, w_out_other, *acts, *ders, gate)


def rows_out_body(act_a, act_b, wa, wb, gate, out):
    o = jnp.dot(act_a[...], wa[...], preferred_element_type=jnp.float32)
    o += jnp.dot(act_b[...], wb[...], preferred_element_type=jnp.float32)
    o = (o * gate[...]).astype(out.dtype)
    for f in range(out.shape[0]):
        out[f] = o[:, f * WIDTH : (f + 1) * WIDTH]


def rows_out(acts, w_out, w_out_other, gate):
    per = 2
    a_spec = pl.BlockSpec((ROWS, UNITS), lambda i: (0, 0))
    w_spec = pl.BlockSpec((UNITS, per * WIDTH), lambda i: (0, i))
    return pl.pallas_call(
        rows_out_body,
        grid=(SLICES // per,),
        out_shape=jax.ShapeDtypeStruct((SLICES, ROWS, WIDTH), jnp.bfloat16),
        in_specs=[a_spec, a_spec, w_spec, w_spec, pl.BlockSpec((ROWS, 1), lambda i: (0, 0))],
        out_specs=pl.BlockSpec((per, ROWS, WIDTH), lambda i: (i, 0, 0)),
        compiler_params=params(),
        cost_estimate=cost(2 * ROWS * D * 2 * UNITS, 21 * MIB),
        name="rows_out",
    )(*acts, w_out, w_out_other, gate)


def rows_grad_body(tiles, dh_a, dh_b, wa, wb, out):
    dims = (((1,), (1,)), ((), ()))
    r = lax.dot_general(dh_a[...], wa[...], dims, preferred_element_type=jnp.float32)
    r += lax.dot_general(dh_b[...], wb[...], dims, preferred_element_type=jnp.float32)
    r = r.astype(out.dtype)
    out[...] = jnp.zeros_like(out)
    for s in range(OWN):
        for f in range(out.shape[1]):
            out[tiles[s], f] = r[s * BLK : (s + 1) * BLK, f * WIDTH : (f + 1) * WIDTH]


def rows_grad(tiles, dhs, w_in, w_in_other, tile_count):
    per = 2
    a_spec = pl.BlockSpec((ROWS, UNITS), lambda i: (0, 0))
    w_spec = pl.BlockSpec((per * WIDTH, UNITS), lambda i: (i, 0))
    return pl.pallas_call(
        rows_grad_body,
        grid=(SLICES // per,),
        out_shape=jax.ShapeDtypeStruct((tile_count, SLICES, BLK, WIDTH), jnp.bfloat16),
        in_specs=[SMEM, a_spec, a_spec, w_spec, w_spec],
        out_specs=pl.BlockSpec((tile_count, per, BLK, WIDTH), lambda i: (0, i, 0, 0)),
        compiler_params=params(),
        cost_estimate=cost(2 * ROWS * D * 2 * UNITS, 27 * MIB),
        name="rows_grad",
    )(tiles, *dhs, w_in, w_in_other)


def merge_body(count, ids, parts, out, total):
    total[...] = jnp.zeros_like(total)

    def step(i, carry):
        total[ids[i]] += parts[i].astype(jnp.float32)
        return carry

    lax.fori_loop(0, count, step, 0)
    out[...] = total[: out.shape[0]].astype(out.dtype)


def merge(parts, ids, blocks):
    count = parts.shape[0]
    return pl.pallas_call(
        functools.partial(merge_body, count),
        out_shape=jax.ShapeDtypeStruct((blocks, BLK, WIDTH), jnp.bfloat16),
        in_specs=[SMEM, VMEM],
        out_specs=VMEM,
        scratch_shapes=[pltpu.VMEM((blocks + 1, BLK, WIDTH), jnp.float32)],
        compiler_params=params(),
        cost_estimate=cost(0, (count + blocks) * BLK * WIDTH * 2 * 2),
        name="merge",
    )(ids, parts)


def exchange(value):
    return lax.all_to_all(value, "exp", split_axis=0, concat_axis=0, tiled=True)


def on_device(tokens, cotangent, gates, picks, w_in, w_out):
    tile_count = lax.axis_size("tok")
    my_tile = lax.axis_index("tok")
    my_expert = lax.axis_index("exp")
    core = my_tile % 2
    blocks = tokens.shape[0] // BLK
    experts = gates.shape[1]
    w_in, w_out = w_in[0], w_out[0]
    pairs = [(i, i ^ 1) for i in range(tile_count)]
    w_in_other = lax.ppermute(w_in, "tok", pairs)
    w_out_other = lax.ppermute(w_out, "tok", pairs)

    chosen = picks < blocks
    order = jnp.arange(tile_count, dtype=jnp.int32)
    rank = jnp.sum(
        jnp.where((order[None, :] < order[:, None])[:, :, None], chosen[None], False).astype(
            jnp.int32
        ),
        axis=1,
    )
    slot = jnp.arange(CAP, dtype=jnp.int32)
    at_slot = (chosen & (rank >= 0))[:, :, None] & (rank[:, :, None] == slot)
    slot_tile = jnp.sum(jnp.where(at_slot, order[:, None, None], 0), axis=0)
    slot_block = jnp.sum(jnp.where(at_slot, picks[:, :, None], 0), axis=0)
    slot_row = slot_tile * blocks + slot_block
    own_rows = lax.dynamic_slice_in_dim(slot_row, core * OWN, OWN, 1)
    own_tiles = lax.dynamic_slice(slot_tile, (my_expert, core * OWN), (1, OWN))[0]
    my_rows = lax.dynamic_index_in_dim(own_rows, my_expert, 0, False)
    tile_picks = lax.dynamic_index_in_dim(picks, my_tile, 0, False)

    cot_all = lax.all_gather(cotangent.reshape(blocks, BLK, WIDTH), "tok", tiled=True)
    gate_mine = lax.dynamic_index_in_dim(gates, my_expert, 1, False).reshape(blocks, BLK)
    gate_all = lax.all_gather(gate_mine, "tok", tiled=True)
    gate = jnp.take(gate_all, my_rows, axis=0, mode="clip").reshape(ROWS, 1)
    dy = exchange(pick_blocks(cot_all, own_rows.reshape(-1)).reshape(experts, ROWS, WIDTH))

    x_slot = pick_blocks(tokens.reshape(blocks, BLK, WIDTH), jnp.minimum(tile_picks, blocks - 1))
    x_all = lax.all_gather(exchange(x_slot), "tok")

    act_a, act_b, der_a, der_b = hidden(own_tiles, x_all, w_in, w_in_other)
    dh_a, dh_b, dgate = back(dy, w_out, w_out_other, (act_a, act_b), (der_a, der_b), gate)
    dx_all = rows_grad(own_tiles, (dh_a, dh_b), w_in, w_in_other, tile_count)
    out_rows = rows_out((act_a, act_b), w_out, w_out_other, gate)

    dx = lax.psum_scatter(dx_all, "tok", scatter_dimension=0)
    d_tokens = merge(exchange(dx), tile_picks, blocks)

    parts = exchange(out_rows).reshape(experts * OWN, BLK, WIDTH)
    mixed_all = merge(parts, own_rows.reshape(-1), tile_count * blocks)
    mixed = lax.psum_scatter(
        mixed_all.reshape(tile_count, blocks * BLK, WIDTH), "tok", scatter_dimension=0
    )

    spread = jnp.zeros((experts, CAP, BLK), jnp.float32)
    spread = lax.dynamic_update_slice(
        spread, dgate.reshape(1, OWN, BLK), (my_expert, core * OWN, jnp.int32(0))
    )
    grads = lax.psum(spread, ("tok", "exp"))
    here = slot_tile == my_tile
    here &= slot[None, :] < CAP
    taken = lax.dynamic_index_in_dim(chosen, my_tile, 0, False)
    mine = jnp.sum(jnp.where((here & taken[:, None])[:, :, None], grads, 0.0), axis=1)
    at_block = tile_picks[None, :] == jnp.arange(blocks, dtype=jnp.int32)[:, None]
    d_gates = jnp.where(at_block[:, None, :], mine.T[None], 0.0)
    return (
        mixed,
        d_tokens.reshape(blocks * BLK, WIDTH),
        d_gates.reshape(blocks * BLK, experts),
    )


def solution(mesh):
    return jax.shard_map(
        on_device,
        mesh=mesh,
        in_specs=(
            P("tok", "exp"),
            P("tok", "exp"),
            P("tok", None),
            P(),
            P("exp", None, "tok"),
            P("exp", "tok", None),
        ),
        out_specs=(P("tok", "exp"), P("tok", "exp"), P("tok", None)),
        check_vma=False,
    )
```

```python
import functools

import jax
import jax.numpy as jnp
from jax import lax
from jax.experimental import pallas as pl
from jax.experimental.pallas import tpu as pltpu
from jax.sharding import PartitionSpec as P

D = 4096
BLK = 128
WIDTH = 256
SLICES = D // WIDTH
CAP = 6
OWN = CAP // 2
ROWS = OWN * BLK
UNITS = 1024
GELU_C = 0.7978845608028654
GELU_K = 0.044715
MIB = 1024 * 1024
PICK_MIB, HID_MIB, BACK_MIB, OUT_MIB, MERGE_MIB = 60, 60, 60, 60, 60
ANY = pl.BlockSpec(memory_space=pl.ANY)
SMEM = pl.BlockSpec(memory_space=pltpu.SMEM)
VMEM = pl.BlockSpec(memory_space=pltpu.VMEM)


def params(mib):
    return pltpu.CompilerParams(vmem_limit_bytes=mib * MIB)


def cost(flops, nbytes):
    return pl.CostEstimate(flops=flops, bytes_accessed=nbytes, transcendentals=0)


def pick_body(count, ids, src, out, sems):
    copies = [
        pltpu.make_async_copy(src.at[ids[i]], out.at[i], sems.at[i]) for i in range(count)
    ]
    for copy in copies:
        copy.start()
    for copy in copies:
        copy.wait()


def pick_blocks(src, ids):
    count = ids.shape[0]
    return pl.pallas_call(
        functools.partial(pick_body, count),
        out_shape=jax.ShapeDtypeStruct((count, BLK, WIDTH), src.dtype),
        in_specs=[SMEM, ANY],
        out_specs=VMEM,
        scratch_shapes=[pltpu.SemaphoreType.DMA((count,))],
        compiler_params=params(PICK_MIB),
        cost_estimate=cost(0, 2 * count * BLK * WIDTH * 2),
        name="pick_blocks",
    )(ids, src)


def hidden_body(tiles, x_all, wa, wb, act_a, act_b, der_a, der_b, x_raw, x_v, sems):
    @pl.when(pl.program_id(0) == 0)
    def _():
        copies = [
            pltpu.make_async_copy(x_all.at[tiles[s]], x_raw.at[s], sems.at[s]) for s in range(OWN)
        ]
        for copy in copies:
            copy.start()
        for s in range(OWN):
            copies[s].wait()
            for f in range(SLICES):
                x_v[s * BLK : (s + 1) * BLK, f * WIDTH : (f + 1) * WIDTH] = x_raw[s, f]

    for w, act, der in ((wa, act_a, der_a), (wb, act_b, der_b)):
        h = jnp.dot(x_v[...], w[...], preferred_element_type=jnp.float32)
        sq = h * h
        t = jnp.tanh(h * (GELU_C + (GELU_C * GELU_K) * sq))
        half = 0.5 + 0.5 * t
        act[...] = (h * half).astype(act.dtype)
        slope = 0.5 * GELU_C + (1.5 * GELU_C * GELU_K) * sq
        der[...] = half + (h * slope) * (1.0 - t * t)


def hidden(tiles, x_all, w_in, w_in_other):
    cols = 256
    w_spec = pl.BlockSpec((D, cols), lambda i: (0, i))
    o_spec = pl.BlockSpec((ROWS, cols), lambda i: (0, i))
    act = jax.ShapeDtypeStruct((ROWS, UNITS), jnp.bfloat16)
    der = jax.ShapeDtypeStruct((ROWS, UNITS), jnp.float32)
    return pl.pallas_call(
        hidden_body,
        grid=(UNITS // cols,),
        out_shape=(act, act, der, der),
        in_specs=[SMEM, ANY, w_spec, w_spec],
        out_specs=(o_spec, o_spec, o_spec, o_spec),
        scratch_shapes=[
            pltpu.VMEM((OWN, SLICES, BLK, WIDTH), jnp.bfloat16),
            pltpu.VMEM((ROWS, D), jnp.bfloat16),
            pltpu.SemaphoreType.DMA((OWN,)),
        ],
        compiler_params=params(HID_MIB),
        cost_estimate=cost(2 * ROWS * D * 2 * UNITS, 24 * MIB),
        name="hidden",
    )(tiles, x_all, w_in, w_in_other)


def back_body(
    first, tiles, dy, oa, ob, ia, ib, act_a, act_b, der_a, der_b, gate, out, dgate, g_v, dh_a, dh_b
):
    step = pl.program_id(0)
    dims = (((1,), (1,)), ((), ()))

    @pl.when(step == 0)
    def _():
        scale = gate[...]
        for f in range(SLICES):
            g = scale * dy[f].astype(jnp.float32)
            g_v[:, f * WIDTH : (f + 1) * WIDTH] = g.astype(g_v.dtype)
        dgate[...] = jnp.zeros_like(dgate)

    @pl.when(step < first)
    def _():
        total = dgate[...]
        cols = oa.shape[0]
        here = pl.ds(pl.multiple_of(step * cols, cols), cols)
        for w, act, der, dh in ((oa, act_a, der_a, dh_a), (ob, act_b, der_b, dh_b)):
            u = lax.dot_general(g_v[...], w[...], dims, preferred_element_type=jnp.float32)
            dh[:, here] = (u * der[...]).astype(dh.dtype)
            total += jnp.sum(act[...].astype(jnp.float32) * u, axis=1, keepdims=True)
        dgate[...] = jnp.where(step == first - 1, total / gate[...], total)

    @pl.when(step >= first)
    def _():
        r = lax.dot_general(dh_a[...], ia[...], dims, preferred_element_type=jnp.float32)
        r += lax.dot_general(dh_b[...], ib[...], dims, preferred_element_type=jnp.float32)
        r = r.astype(out.dtype)
        out[...] = jnp.zeros_like(out)
        for s in range(OWN):
            for f in range(out.shape[1]):
                out[tiles[s], f] = r[s * BLK : (s + 1) * BLK, f * WIDTH : (f + 1) * WIDTH]


def back(tiles, dy, w_out, w_out_other, w_in, w_in_other, acts, ders, gate, tile_count):
    cols, per = 256, 4
    first, second = UNITS // cols, SLICES // per
    early = lambda i: jnp.minimum(i, first - 1)
    late = lambda i: jnp.maximum(i - first, 0)
    wo_spec = pl.BlockSpec((cols, D), lambda i: (early(i), 0))
    wi_spec = pl.BlockSpec((per * WIDTH, UNITS), lambda i: (late(i), 0))
    h_spec = pl.BlockSpec((ROWS, cols), lambda i: (0, early(i)))
    g_spec = pl.BlockSpec((ROWS, 1), lambda i: (0, 0))
    dy_spec = pl.BlockSpec((SLICES, ROWS, WIDTH), lambda i: (0, 0, 0))
    return pl.pallas_call(
        functools.partial(back_body, first),
        grid=(first + second,),
        out_shape=(
            jax.ShapeDtypeStruct((tile_count, SLICES, BLK, WIDTH), jnp.bfloat16),
            jax.ShapeDtypeStruct((ROWS, 1), jnp.float32),
        ),
        in_specs=[SMEM, dy_spec, wo_spec, wo_spec, wi_spec, wi_spec]
        + [h_spec] * 4
        + [g_spec],
        out_specs=(
            pl.BlockSpec((tile_count, per, BLK, WIDTH), lambda i: (0, late(i), 0, 0)),
            g_spec,
        ),
        scratch_shapes=[
            pltpu.VMEM((ROWS, D), jnp.bfloat16),
            pltpu.VMEM((ROWS, UNITS), jnp.bfloat16),
            pltpu.VMEM((ROWS, UNITS), jnp.bfloat16),
        ],
        compiler_params=params(BACK_MIB),
        cost_estimate=cost(4 * ROWS * D * 2 * UNITS, 50 * MIB),
        name="back",
    )(tiles, dy, w_out, w_out_other, w_in, w_in_other, *acts, *ders, gate)


def rows_out_body(act_a, act_b, wa, wb, gate, out):
    o = jnp.dot(act_a[...], wa[...], preferred_element_type=jnp.float32)
    o += jnp.dot(act_b[...], wb[...], preferred_element_type=jnp.float32)
    o = (o * gate[...]).astype(out.dtype)
    for f in range(out.shape[0]):
        out[f] = o[:, f * WIDTH : (f + 1) * WIDTH]


def rows_out(acts, w_out, w_out_other, gate):
    per = 4
    a_spec = pl.BlockSpec((ROWS, UNITS), lambda i: (0, 0))
    w_spec = pl.BlockSpec((UNITS, per * WIDTH), lambda i: (0, i))
    return pl.pallas_call(
        rows_out_body,
        grid=(SLICES // per,),
        out_shape=jax.ShapeDtypeStruct((SLICES, ROWS, WIDTH), jnp.bfloat16),
        in_specs=[a_spec, a_spec, w_spec, w_spec, pl.BlockSpec((ROWS, 1), lambda i: (0, 0))],
        out_specs=pl.BlockSpec((per, ROWS, WIDTH), lambda i: (i, 0, 0)),
        compiler_params=params(OUT_MIB),
        cost_estimate=cost(2 * ROWS * D * 2 * UNITS, 21 * MIB),
        name="rows_out",
    )(*acts, w_out, w_out_other, gate)


def merge_body(count, ids, parts, out, total):
    total[...] = jnp.zeros_like(total)

    def step(i, carry):
        total[ids[i]] += parts[i].astype(jnp.float32)
        return carry

    lax.fori_loop(0, count, step, 0)
    out[...] = total[: out.shape[0]].astype(out.dtype)


def merge(parts, ids, blocks):
    count = parts.shape[0]
    return pl.pallas_call(
        functools.partial(merge_body, count),
        out_shape=jax.ShapeDtypeStruct((blocks, BLK, WIDTH), jnp.bfloat16),
        in_specs=[SMEM, VMEM],
        out_specs=VMEM,
        scratch_shapes=[pltpu.VMEM((blocks + 1, BLK, WIDTH), jnp.float32)],
        compiler_params=params(MERGE_MIB),
        cost_estimate=cost(0, (count + blocks) * BLK * WIDTH * 2 * 2),
        name="merge",
    )(ids, parts)


def exchange(value):
    return lax.all_to_all(value, "exp", split_axis=0, concat_axis=0, tiled=True)


def along_z(value, hops, chips):
    pairs = [
        (2 * ((z + hops) % chips) + core, 2 * z + core) for z in range(chips) for core in range(2)
    ]
    return lax.ppermute(value, "tok", pairs)


def other_core(value, chips):
    return lax.ppermute(value, "tok", [(i, i ^ 1) for i in range(2 * chips)])


def on_device(tokens, cotangent, gates, picks, w_in, w_out):
    tile_count = lax.axis_size("tok")
    chips = tile_count // 2
    my_tile = lax.axis_index("tok")
    my_expert = lax.axis_index("exp")
    core = my_tile % 2
    blocks = tokens.shape[0] // BLK
    experts = gates.shape[1]
    w_in, w_out = w_in[0], w_out[0]

    cot_all = lax.all_gather(cotangent.reshape(blocks, BLK, WIDTH), "tok", tiled=True)
    tile_picks = lax.dynamic_index_in_dim(picks, my_tile, 0, False)
    x_slot = pick_blocks(tokens.reshape(blocks, BLK, WIDTH), jnp.minimum(tile_picks, blocks - 1))
    x_all = lax.all_gather(exchange(x_slot), "tok")

    chosen = picks < blocks
    order = jnp.arange(tile_count, dtype=jnp.int32)
    before = (order[None, :] < order[:, None])[:, :, None] & chosen[None]
    rank = jnp.sum(before.astype(jnp.int32), axis=1)
    slot = jnp.arange(CAP, dtype=jnp.int32)
    at_slot = chosen[:, :, None] & (rank[:, :, None] == slot)
    slot_tile = jnp.sum(jnp.where(at_slot, order[:, None, None], 0), axis=0)
    slot_block = jnp.sum(jnp.where(at_slot, picks[:, :, None], 0), axis=0)
    slot_place = (slot_tile // 2 - my_tile // 2) % chips + chips * ((slot_tile + core) % 2)

    def own_of(values):
        return lax.dynamic_slice_in_dim(values, core * OWN, OWN, 1)

    own_rows = own_of(slot_tile * blocks + slot_block)
    own_places = own_of(slot_place * blocks + slot_block)
    own_tiles = lax.dynamic_index_in_dim(own_of(slot_tile), my_expert, 0, False)
    my_places = lax.dynamic_index_in_dim(own_places, my_expert, 0, False)

    gate_mine = lax.dynamic_index_in_dim(gates, my_expert, 1, False).reshape(blocks, BLK)
    gate_near = jnp.concatenate([gate_mine] + [along_z(gate_mine, k, chips) for k in (1, 2, 3)])
    gate_all = jnp.concatenate([gate_near, other_core(gate_near, chips)])
    gate = jnp.take(gate_all, my_places, axis=0, mode="clip").reshape(ROWS, 1)

    dy = exchange(pick_blocks(cot_all, own_rows.reshape(-1)).reshape(experts, ROWS, WIDTH))
    w_in_other = other_core(w_in, chips)
    w_out_other = other_core(w_out, chips)

    act_a, act_b, der_a, der_b = hidden(own_tiles, x_all, w_in, w_in_other)
    dx_all, dgate = back(
        own_tiles, dy, w_out, w_out_other, w_in, w_in_other,
        (act_a, act_b), (der_a, der_b), gate, tile_count,
    )
    out_rows = rows_out((act_a, act_b), w_out, w_out_other, gate)

    dx = lax.psum_scatter(dx_all, "tok", scatter_dimension=0)

    parts = exchange(out_rows).reshape(experts * OWN, BLK, WIDTH)
    mixed_all = merge(parts, own_rows.reshape(-1), tile_count * blocks)
    mixed = lax.psum_scatter(
        mixed_all.reshape(tile_count, blocks * BLK, WIDTH), "tok", scatter_dimension=0
    )
    dx = exchange(dx)
    d_tokens = merge(dx, tile_picks, blocks)

    dgate = dgate.reshape(OWN, BLK)
    dgate += sum(along_z(dgate, k, chips) for k in (1, 2, 3))
    theirs = other_core(dgate, chips)
    low = jnp.where(core == 0, dgate, theirs)
    high = jnp.where(core == 0, theirs, dgate)
    both = jnp.concatenate([low, high])
    both, _ = lax.optimization_barrier((both, dx))
    grads = exchange(jnp.broadcast_to(both[None], (experts, CAP, BLK)))
    taken = lax.dynamic_index_in_dim(chosen, my_tile, 0, False)
    here = (slot_tile == my_tile) & taken[:, None]
    mine = jnp.sum(jnp.where(here[:, :, None], grads, 0.0), axis=1)
    at_block = tile_picks[None, :] == jnp.arange(blocks, dtype=jnp.int32)[:, None]
    d_gates = jnp.where(at_block[:, None, :], mine.T[None], 0.0)
    return (
        mixed,
        d_tokens.reshape(blocks * BLK, WIDTH),
        d_gates.reshape(blocks * BLK, experts),
    )


def solution(mesh):
    return jax.shard_map(
        on_device,
        mesh=mesh,
        in_specs=(
            P("tok", "exp"),
            P("tok", "exp"),
            P("tok", None),
            P(),
            P("exp", None, "tok"),
            P("exp", "tok", None),
        ),
        out_specs=(P("tok", "exp"), P("tok", "exp"), P("tok", None)),
        check_vma=False,
    )
```

```python
import functools

import jax
import jax.numpy as jnp
from jax import lax
from jax.experimental import pallas as pl
from jax.experimental.pallas import tpu as pltpu
from jax.sharding import PartitionSpec as P

D = 4096
BLK = 128
WIDTH = 256
SLICES = D // WIDTH
CAP = 6
OWN = CAP // 2
ROWS = OWN * BLK
UNITS = 1024
GELU_C = 0.7978845608028654
GELU_K = 0.044715
MIB = 1024 * 1024
HID_COST = 2
PICK_MIB, HID_MIB, BACK_MIB, OUT_MIB, MERGE_MIB = 60, 60, 60, 60, 60
ANY = pl.BlockSpec(memory_space=pl.ANY)
SMEM = pl.BlockSpec(memory_space=pltpu.SMEM)
VMEM = pl.BlockSpec(memory_space=pltpu.VMEM)


def params(mib):
    return pltpu.CompilerParams(vmem_limit_bytes=mib * MIB)


def cost(flops, nbytes):
    return pl.CostEstimate(flops=flops, bytes_accessed=nbytes, transcendentals=0)


def pick_body(count, ids, src, out, sems):
    copies = [
        pltpu.make_async_copy(src.at[ids[i]], out.at[i], sems.at[i]) for i in range(count)
    ]
    for copy in copies:
        copy.start()
    for copy in copies:
        copy.wait()


def pick_blocks(src, ids):
    count = ids.shape[0]
    return pl.pallas_call(
        functools.partial(pick_body, count),
        out_shape=jax.ShapeDtypeStruct((count, BLK, WIDTH), src.dtype),
        in_specs=[SMEM, ANY],
        out_specs=VMEM,
        scratch_shapes=[pltpu.SemaphoreType.DMA((count,))],
        compiler_params=params(PICK_MIB),
        cost_estimate=cost(0, 2 * count * BLK * WIDTH * 2),
        name="pick_blocks",
    )(ids, src)


def start(copies):
    for copy in copies:
        copy.start()


def wait(copies):
    for copy in copies:
        copy.wait()


GROUP = 512
HALF = GROUP // 2
CHIP_UNITS = 2 * UNITS
STEPS = CHIP_UNITS // GROUP
PART = SLICES // 2


def hidden_body(sources, picked, *refs):
    srcs = refs[:sources]
    wa, wb, act, der, x_raw, x_v, w_v, x_sems, w_sems = refs[sources:]
    step = pl.program_id(0)

    def weights(i):
        cols = pl.ds(pl.multiple_of(i * HALF, HALF), HALF)
        slot = i % 2
        return [
            pltpu.make_async_copy(
                w.at[:, cols], w_v.at[slot, :, pl.ds(k * HALF, HALF)], w_sems.at[slot, k]
            )
            for k, w in enumerate((wa, wb))
        ]

    @pl.when(step == 0)
    def _():
        for s in range(OWN):
            for side in range(2):
                own, above, below, far_a, far_b = srcs[5 * side : 5 * side + 5]
                for hops, source in ((0, own), (1, above), (3, below)):

                    @pl.when(picked[s] == 4 * side + hops)
                    def _(s=s, source=source):
                        pltpu.make_async_copy(source, x_raw.at[s], x_sems.at[s]).start()

                @pl.when(picked[s] == 4 * side + 2)
                def _(s=s, far_a=far_a, far_b=far_b):
                    for source, at in ((far_a, 0), (far_b, PART)):
                        to = x_raw.at[s, pl.ds(at, PART)]
                        pltpu.make_async_copy(source, to, x_sems.at[s]).start()

        start(weights(0))
        for s in range(OWN):
            pltpu.make_async_copy(srcs[0], x_raw.at[s], x_sems.at[s]).wait()
            for f in range(SLICES):
                x_v[s * BLK : (s + 1) * BLK, f * WIDTH : (f + 1) * WIDTH] = x_raw[s, f]

    @pl.when(step + 1 < STEPS)
    def _():
        start(weights(step + 1))

    wait(weights(step))
    h = jnp.dot(x_v[...], w_v[step % 2], preferred_element_type=jnp.float32)
    sq = h * h
    t = jnp.tanh(h * (GELU_C + (GELU_C * GELU_K) * sq))
    half = 0.5 + 0.5 * t
    act[...] = (h * half).astype(act.dtype)
    slope = 0.5 * GELU_C + (1.5 * GELU_C * GELU_K) * sq
    der[...] = half + (h * slope) * (1.0 - t * t)


def hidden(picked, srcs, w_in, w_in_other):
    o_spec = pl.BlockSpec((ROWS, GROUP), lambda i: (0, i))
    return pl.pallas_call(
        functools.partial(hidden_body, len(srcs)),
        grid=(STEPS,),
        out_shape=(
            jax.ShapeDtypeStruct((ROWS, CHIP_UNITS), jnp.bfloat16),
            jax.ShapeDtypeStruct((ROWS, CHIP_UNITS), jnp.float32),
        ),
        in_specs=[SMEM] + [ANY] * (len(srcs) + 2),
        out_specs=(o_spec, o_spec),
        scratch_shapes=[
            pltpu.VMEM((OWN, SLICES, BLK, WIDTH), jnp.bfloat16),
            pltpu.VMEM((ROWS, D), jnp.bfloat16),
            pltpu.VMEM((2, D, GROUP), jnp.bfloat16),
            pltpu.SemaphoreType.DMA((OWN,)),
            pltpu.SemaphoreType.DMA((2, 2)),
        ],
        compiler_params=params(HID_MIB),
        cost_estimate=cost(HID_COST * 2 * ROWS * D * 2 * UNITS, 24 * MIB),
        name="hidden",
    )(picked, *srcs, w_in, w_in_other)


def back_body(
    feats, tiles, dy, oa, ob, ia, ib, act, der, gate, out, dgate,
    dy_v, g_v, o_v, i_v, dh, dy_sem, o_sems, i_sems,
):
    step = pl.program_id(0)
    last = pl.num_programs(0) - 1
    dims = (((1,), (1,)), ((), ()))

    def out_weights(i):
        rows = pl.ds(pl.multiple_of(i * HALF, HALF), HALF)
        slot = i % 2
        return [
            pltpu.make_async_copy(
                w.at[rows, :], o_v.at[slot, pl.ds(k * HALF, HALF), :], o_sems.at[slot, k]
            )
            for k, w in enumerate((oa, ob))
        ]

    def in_weights(i):
        rows = pl.ds(pl.multiple_of(i * feats, feats), feats)
        slot = i % 2
        return [
            pltpu.make_async_copy(
                w.at[rows, pl.ds(j * HALF, HALF)],
                i_v.at[slot, :, pl.ds(j * GROUP + k * HALF, HALF)],
                i_sems.at[slot, k, j],
            )
            for k, w in enumerate((ia, ib))
            for j in range(STEPS)
        ]

    @pl.when(step == 0)
    def _():
        whole = pltpu.make_async_copy(dy, dy_v, dy_sem)
        whole.start()
        start(out_weights(0))
        whole.wait()
        scale = gate[...]
        for f in range(SLICES):
            g = scale * dy_v[f].astype(jnp.float32)
            g_v[:, f * WIDTH : (f + 1) * WIDTH] = g.astype(g_v.dtype)
        dgate[...] = jnp.zeros_like(dgate)

    @pl.when(step < STEPS)
    def _():
        @pl.when(step + 1 < STEPS)
        def _():
            start(out_weights(step + 1))

        @pl.when(step + 1 == STEPS)
        def _():
            start(in_weights(0))

        wait(out_weights(step))
        u = lax.dot_general(g_v[...], o_v[step % 2], dims, preferred_element_type=jnp.float32)
        here = pl.ds(pl.multiple_of(step * GROUP, GROUP), GROUP)
        dh[:, here] = (u * der[...]).astype(dh.dtype)
        total = dgate[...] + jnp.sum(act[...].astype(jnp.float32) * u, axis=1, keepdims=True)
        dgate[...] = jnp.where(step == STEPS - 1, total / gate[...], total)

    @pl.when(step >= STEPS)
    def _():
        i = step - STEPS

        @pl.when(step < last)
        def _():
            start(in_weights(i + 1))

        wait(in_weights(i))
        r = lax.dot_general(dh[...], i_v[i % 2], dims, preferred_element_type=jnp.float32)
        r = r.astype(out.dtype)
        out[...] = jnp.zeros_like(out)
        for s in range(OWN):
            for f in range(out.shape[1]):
                out[tiles[s], f] = r[s * BLK : (s + 1) * BLK, f * WIDTH : (f + 1) * WIDTH]


def back(tiles, dy, w_out, w_out_other, w_in, w_in_other, act, der, gate, tile_count):
    per = 4
    feats = per * WIDTH
    h_spec = pl.BlockSpec((ROWS, GROUP), lambda i: (0, jnp.minimum(i, STEPS - 1)))
    g_spec = pl.BlockSpec((ROWS, 1), lambda i: (0, 0))
    return pl.pallas_call(
        functools.partial(back_body, feats),
        grid=(STEPS + SLICES // per,),
        out_shape=(
            jax.ShapeDtypeStruct((tile_count, SLICES, BLK, WIDTH), jnp.bfloat16),
            jax.ShapeDtypeStruct((ROWS, 1), jnp.float32),
        ),
        in_specs=[SMEM, ANY, ANY, ANY, ANY, ANY, h_spec, h_spec, g_spec],
        out_specs=(
            pl.BlockSpec(
                (tile_count, per, BLK, WIDTH), lambda i: (0, jnp.maximum(i - STEPS, 0), 0, 0)
            ),
            g_spec,
        ),
        scratch_shapes=[
            pltpu.VMEM((SLICES, ROWS, WIDTH), jnp.bfloat16),
            pltpu.VMEM((ROWS, D), jnp.bfloat16),
            pltpu.VMEM((2, GROUP, D), jnp.bfloat16),
            pltpu.VMEM((2, feats, CHIP_UNITS), jnp.bfloat16),
            pltpu.VMEM((ROWS, CHIP_UNITS), jnp.bfloat16),
            pltpu.SemaphoreType.DMA,
            pltpu.SemaphoreType.DMA((2, 2)),
            pltpu.SemaphoreType.DMA((2, 2, STEPS)),
        ],
        compiler_params=params(BACK_MIB),
        cost_estimate=cost(4 * ROWS * D * 2 * UNITS, 50 * MIB),
        name="back",
    )(tiles, dy, w_out, w_out_other, w_in, w_in_other, act, der, gate)


def rows_out_body(feats, act, wa, wb, gate, out, w_v, sems):
    step = pl.program_id(0)

    def weights(i):
        cols = pl.ds(pl.multiple_of(i * feats, feats), feats)
        slot = i % 2
        return [
            pltpu.make_async_copy(
                w.at[pl.ds(j * HALF, HALF), cols],
                w_v.at[slot, pl.ds(j * GROUP + k * HALF, HALF), :],
                sems.at[slot, k, j],
            )
            for k, w in enumerate((wa, wb))
            for j in range(STEPS)
        ]

    @pl.when(step == 0)
    def _():
        start(weights(0))

    @pl.when(step + 1 < pl.num_programs(0))
    def _():
        start(weights(step + 1))

    wait(weights(step))
    o = jnp.dot(act[...], w_v[step % 2], preferred_element_type=jnp.float32)
    o = (o * gate[...]).astype(out.dtype)
    for f in range(out.shape[0]):
        out[f] = o[:, f * WIDTH : (f + 1) * WIDTH]


def rows_out(act, w_out, w_out_other, gate):
    per = 4
    feats = per * WIDTH
    return pl.pallas_call(
        functools.partial(rows_out_body, feats),
        grid=(SLICES // per,),
        out_shape=jax.ShapeDtypeStruct((SLICES, ROWS, WIDTH), jnp.bfloat16),
        in_specs=[
            pl.BlockSpec((ROWS, CHIP_UNITS), lambda i: (0, 0)),
            ANY,
            ANY,
            pl.BlockSpec((ROWS, 1), lambda i: (0, 0)),
        ],
        out_specs=pl.BlockSpec((per, ROWS, WIDTH), lambda i: (i, 0, 0)),
        scratch_shapes=[
            pltpu.VMEM((2, CHIP_UNITS, feats), jnp.bfloat16),
            pltpu.SemaphoreType.DMA((2, 2, STEPS)),
        ],
        compiler_params=params(OUT_MIB),
        cost_estimate=cost(2 * ROWS * D * 2 * UNITS, 21 * MIB),
        name="rows_out",
    )(act, w_out, w_out_other, gate)


def merge_body(count, ids, parts, out, total):
    total[...] = jnp.zeros_like(total)

    def step(i, carry):
        total[ids[i]] += parts[i].astype(jnp.float32)
        return carry

    lax.fori_loop(0, count, step, 0)
    out[...] = total[: out.shape[0]].astype(out.dtype)


def merge(parts, ids, blocks):
    count = parts.shape[0]
    return pl.pallas_call(
        functools.partial(merge_body, count),
        out_shape=jax.ShapeDtypeStruct((blocks, BLK, WIDTH), jnp.bfloat16),
        in_specs=[SMEM, VMEM],
        out_specs=VMEM,
        scratch_shapes=[pltpu.VMEM((blocks + 1, BLK, WIDTH), jnp.float32)],
        compiler_params=params(MERGE_MIB),
        cost_estimate=cost(0, (count + blocks) * BLK * WIDTH * 2 * 2),
        name="merge",
    )(ids, parts)


def exchange(value):
    return lax.all_to_all(value, "exp", split_axis=0, concat_axis=0, tiled=True)


def along_z(value, hops, chips):
    pairs = [
        (2 * ((z + hops) % chips) + core, 2 * z + core) for z in range(chips) for core in range(2)
    ]
    return lax.ppermute(value, "tok", pairs)


def other_core(value, chips):
    return lax.ppermute(value, "tok", [(i, i ^ 1) for i in range(2 * chips)])


def on_device(tokens, cotangent, gates, picks, w_in, w_out):
    tile_count = lax.axis_size("tok")
    chips = tile_count // 2
    my_tile = lax.axis_index("tok")
    my_expert = lax.axis_index("exp")
    core = my_tile % 2
    blocks = tokens.shape[0] // BLK
    experts = gates.shape[1]
    w_in, w_out = w_in[0], w_out[0]

    cot_all = lax.all_gather(cotangent.reshape(blocks, BLK, WIDTH), "tok", tiled=True)
    tile_picks = lax.dynamic_index_in_dim(picks, my_tile, 0, False)
    x_slot = pick_blocks(tokens.reshape(blocks, BLK, WIDTH), jnp.minimum(tile_picks, blocks - 1))
    x_mine = exchange(x_slot)

    chosen = picks < blocks
    order = jnp.arange(tile_count, dtype=jnp.int32)
    before = (order[None, :] < order[:, None])[:, :, None] & chosen[None]
    rank = jnp.sum(before.astype(jnp.int32), axis=1)
    slot = jnp.arange(CAP, dtype=jnp.int32)
    at_slot = chosen[:, :, None] & (rank[:, :, None] == slot)
    slot_tile = jnp.sum(jnp.where(at_slot, order[:, None, None], 0), axis=0)
    slot_block = jnp.sum(jnp.where(at_slot, picks[:, :, None], 0), axis=0)
    slot_place = (slot_tile // 2 - my_tile // 2) % chips + chips * ((slot_tile + core) % 2)

    def own_of(values):
        return lax.dynamic_slice_in_dim(values, core * OWN, OWN, 1)

    own_rows = own_of(slot_tile * blocks + slot_block)
    own_places = own_of(slot_place * blocks + slot_block)
    own_tiles = lax.dynamic_index_in_dim(own_of(slot_tile), my_expert, 0, False)
    my_places = lax.dynamic_index_in_dim(own_places, my_expert, 0, False)
    my_rows = lax.dynamic_index_in_dim(own_rows, my_expert, 0, False)

    gate_mine = lax.dynamic_index_in_dim(gates, my_expert, 1, False).reshape(blocks, BLK)
    gate_all = lax.all_gather(gate_mine, "tok", tiled=True)
    gate = jnp.take(gate_all, my_rows, axis=0, mode="clip").reshape(ROWS, 1)
    places = my_places // blocks
    x_mine, gate, places, own_tiles = lax.optimization_barrier((x_mine, gate, places, own_tiles))
    above, below = along_z(x_mine, 1, chips), along_z(x_mine, 3, chips)
    far = [along_z(above[:PART], 1, chips), along_z(below[PART:], 3, chips)]
    x_near = [x_mine, above, below, *far]
    send_dy = pick_blocks(cot_all, own_rows.reshape(-1))
    dy = exchange(send_dy.reshape(experts, ROWS, WIDTH))
    x_all = x_near + [other_core(piece, chips) for piece in x_near]
    w_in_other = other_core(w_in, chips)
    w_out_other = other_core(w_out, chips)

    act, der = hidden(places, x_all, w_in, w_in_other)
    dx_all, dgate = back(
        own_tiles, dy, w_out, w_out_other, w_in, w_in_other, act, der, gate, tile_count
    )
    out_rows = rows_out(act, w_out, w_out_other, gate)

    dx = lax.psum_scatter(dx_all, "tok", scatter_dimension=0)

    parts = exchange(out_rows).reshape(experts * OWN, BLK, WIDTH)
    mixed_all = merge(parts, own_rows.reshape(-1), tile_count * blocks)
    mixed = lax.psum_scatter(
        mixed_all.reshape(tile_count, blocks * BLK, WIDTH), "tok", scatter_dimension=0
    )
    dx = exchange(dx)
    d_tokens = merge(dx, tile_picks, blocks)

    dgate = dgate.reshape(OWN, BLK)
    dgate += sum(along_z(dgate, k, chips) for k in (1, 2, 3))
    theirs = other_core(dgate, chips)
    low = jnp.where(core == 0, dgate, theirs)
    high = jnp.where(core == 0, theirs, dgate)
    both = jnp.concatenate([low, high])
    both, _ = lax.optimization_barrier((both, dx))
    grads = exchange(jnp.broadcast_to(both[None], (experts, CAP, BLK)))
    taken = lax.dynamic_index_in_dim(chosen, my_tile, 0, False)
    here = (slot_tile == my_tile) & taken[:, None]
    mine = jnp.sum(jnp.where(here[:, :, None], grads, 0.0), axis=1)
    at_block = tile_picks[None, :] == jnp.arange(blocks, dtype=jnp.int32)[:, None]
    d_gates = jnp.where(at_block[:, None, :], mine.T[None], 0.0)
    return (
        mixed,
        d_tokens.reshape(blocks * BLK, WIDTH),
        d_gates.reshape(blocks * BLK, experts),
    )


def solution(mesh):
    return jax.shard_map(
        on_device,
        mesh=mesh,
        in_specs=(
            P("tok", "exp"),
            P("tok", "exp"),
            P("tok", None),
            P(),
            P("exp", None, "tok"),
            P("exp", "tok", None),
        ),
        out_specs=(P("tok", "exp"), P("tok", "exp"), P("tok", None)),
        check_vma=False,
    )
```

```python
import functools

import jax
import jax.numpy as jnp
from jax import lax
from jax.experimental import pallas as pl
from jax.experimental.pallas import tpu as pltpu
from jax.sharding import PartitionSpec as P

D = 4096
BLK = 128
WIDTH = 256
SLICES = D // WIDTH
CAP = 6
OWN = CAP // 2
ROWS = OWN * BLK
UNITS = 1024
GELU_C = 0.7978845608028654
GELU_K = 0.044715
MIB = 1024 * 1024
HID_COST = 2
BACK_COST = 16
PICK_MIB, HID_MIB, BACK_MIB, MERGE_MIB = 60, 60, 62, 60
ANY = pl.BlockSpec(memory_space=pl.ANY)
SMEM = pl.BlockSpec(memory_space=pltpu.SMEM)
VMEM = pl.BlockSpec(memory_space=pltpu.VMEM)


def params(mib):
    return pltpu.CompilerParams(vmem_limit_bytes=mib * MIB)


def cost(flops, nbytes):
    return pl.CostEstimate(flops=flops, bytes_accessed=nbytes, transcendentals=0)


def pick_body(count, ids, src, out, sems):
    copies = [
        pltpu.make_async_copy(src.at[ids[i]], out.at[i], sems.at[i]) for i in range(count)
    ]
    for copy in copies:
        copy.start()
    for copy in copies:
        copy.wait()


def pick_blocks(src, ids):
    count = ids.shape[0]
    return pl.pallas_call(
        functools.partial(pick_body, count),
        out_shape=jax.ShapeDtypeStruct((count, BLK, WIDTH), src.dtype),
        in_specs=[SMEM, ANY],
        out_specs=VMEM,
        scratch_shapes=[pltpu.SemaphoreType.DMA((count,))],
        compiler_params=params(PICK_MIB),
        cost_estimate=cost(0, 2 * count * BLK * WIDTH * 2),
        name="pick_blocks",
    )(ids, src)


def start(copies):
    for copy in copies:
        copy.start()


def wait(copies):
    for copy in copies:
        copy.wait()


GROUP = 512
HALF = GROUP // 2
CHIP_UNITS = 2 * UNITS
STEPS = CHIP_UNITS // GROUP
PART = SLICES // 2


def forward_body(sources, feats, picked, tiles, empty, *refs):
    srcs = refs[:sources]
    (
        ia, ib, oa, ob, gate, act, der, out,
        x_raw, x_v, i_v, o_v, act_v, zero_v, r_v, x_sems, i_sems, o_sems, zero_sems, r_sems,
    ) = refs[sources:]
    step = pl.program_id(0)
    last = pl.num_programs(0) - 1
    per = feats // WIDTH

    def in_weights(i):
        cols = pl.ds(pl.multiple_of(i * HALF, HALF), HALF)
        slot = i % 2
        return [
            pltpu.make_async_copy(
                w.at[:, cols], i_v.at[slot, :, pl.ds(k * HALF, HALF)], i_sems.at[slot, k]
            )
            for k, w in enumerate((ia, ib))
        ]

    def out_weights(i):
        cols = pl.ds(pl.multiple_of(i * feats, feats), feats)
        slot = i % 2
        return [
            pltpu.make_async_copy(
                w.at[pl.ds(j * HALF, HALF), cols],
                o_v.at[slot, pl.ds(j * GROUP + k * HALF, HALF), :],
                o_sems.at[slot, k, j],
            )
            for k, w in enumerate((oa, ob))
            for j in range(STEPS)
        ]

    def zeros():
        return [
            pltpu.make_async_copy(zero_v, out.at[empty[k]], zero_sems.at[k])
            for k in range(zero_sems.shape[0])
        ]

    def results(i):
        here = pl.ds(i * per, per)
        return [
            pltpu.make_async_copy(
                r_v.at[i % 2, s], out.at[tiles[s], here], r_sems.at[i % 2, s]
            )
            for s in range(OWN)
        ]

    @pl.when(step == 0)
    def _():
        for s in range(OWN):
            for side in range(2):
                own, above, below, far_a, far_b = srcs[5 * side : 5 * side + 5]
                for hops, source in ((0, own), (1, above), (3, below)):

                    @pl.when(picked[s] == 4 * side + hops)
                    def _(s=s, source=source):
                        pltpu.make_async_copy(source, x_raw.at[s], x_sems.at[s]).start()

                @pl.when(picked[s] == 4 * side + 2)
                def _(s=s, far_a=far_a, far_b=far_b):
                    for source, at in ((far_a, 0), (far_b, PART)):
                        to = x_raw.at[s, pl.ds(at, PART)]
                        pltpu.make_async_copy(source, to, x_sems.at[s]).start()

        start(in_weights(0))
        zero_v[...] = jnp.zeros_like(zero_v)
        for s in range(OWN):
            pltpu.make_async_copy(srcs[0], x_raw.at[s], x_sems.at[s]).wait()
            for f in range(SLICES):
                x_v[s * BLK : (s + 1) * BLK, f * WIDTH : (f + 1) * WIDTH] = x_raw[s, f]

    for k, zero in enumerate(zeros()):

        @pl.when(step == k + 1)
        def _(zero=zero):
            zero.start()

    @pl.when(step < STEPS)
    def _():
        @pl.when(step + 1 < STEPS)
        def _():
            start(in_weights(step + 1))

        @pl.when(step + 1 == STEPS)
        def _():
            start(out_weights(0))

        wait(in_weights(step))
        h = jnp.dot(x_v[...], i_v[step % 2], preferred_element_type=jnp.float32)
        sq = h * h
        t = jnp.tanh(h * (GELU_C + (GELU_C * GELU_K) * sq))
        half = 0.5 + 0.5 * t
        a = (h * half).astype(act.dtype)
        act[...] = a
        act_v[:, pl.ds(pl.multiple_of(step * GROUP, GROUP), GROUP)] = a
        slope = 0.5 * GELU_C + (1.5 * GELU_C * GELU_K) * sq
        der[...] = half + (h * slope) * (1.0 - t * t)

    @pl.when(step >= STEPS)
    def _():
        i = step - STEPS

        @pl.when(step < last)
        def _():
            start(out_weights(i + 1))

        wait(out_weights(i))

        @pl.when(i >= 2)
        def _():
            wait(results(i - 2))

        o = jnp.dot(act_v[...], o_v[i % 2], preferred_element_type=jnp.float32)
        o = (o * gate[...]).astype(out.dtype)
        for s in range(OWN):
            for f in range(per):
                r_v[i % 2, s, f] = o[s * BLK : (s + 1) * BLK, f * WIDTH : (f + 1) * WIDTH]
        start(results(i))

        @pl.when(step == last)
        def _():
            wait(results(i - 1))
            wait(results(i))
            wait(zeros())


def forward(picked, tiles, empty, srcs, w_in, w_in_other, w_out, w_out_other, gate, tile_count):
    per = 4
    feats = per * WIDTH
    o_spec = pl.BlockSpec((ROWS, GROUP), lambda i: (0, jnp.minimum(i, STEPS - 1)))
    return pl.pallas_call(
        functools.partial(forward_body, len(srcs), feats),
        grid=(STEPS + SLICES // per,),
        out_shape=(
            jax.ShapeDtypeStruct((ROWS, CHIP_UNITS), jnp.bfloat16),
            jax.ShapeDtypeStruct((ROWS, CHIP_UNITS), jnp.float32),
            jax.ShapeDtypeStruct((tile_count, SLICES, BLK, WIDTH), jnp.bfloat16),
        ),
        in_specs=[SMEM] * 3
        + [ANY] * (len(srcs) + 4)
        + [pl.BlockSpec((ROWS, 1), lambda i: (0, 0))],
        out_specs=(o_spec, o_spec, ANY),
        scratch_shapes=[
            pltpu.VMEM((OWN, SLICES, BLK, WIDTH), jnp.bfloat16),
            pltpu.VMEM((ROWS, D), jnp.bfloat16),
            pltpu.VMEM((2, D, GROUP), jnp.bfloat16),
            pltpu.VMEM((2, CHIP_UNITS, feats), jnp.bfloat16),
            pltpu.VMEM((ROWS, CHIP_UNITS), jnp.bfloat16),
            pltpu.VMEM((SLICES, BLK, WIDTH), jnp.bfloat16),
            pltpu.VMEM((2, OWN, per, BLK, WIDTH), jnp.bfloat16),
            pltpu.SemaphoreType.DMA((OWN,)),
            pltpu.SemaphoreType.DMA((2, 2)),
            pltpu.SemaphoreType.DMA((2, 2, STEPS)),
            pltpu.SemaphoreType.DMA((tile_count - OWN,)),
            pltpu.SemaphoreType.DMA((2, OWN)),
        ],
        compiler_params=params(HID_MIB),
        cost_estimate=cost(HID_COST * 2 * ROWS * D * 2 * UNITS, 24 * MIB),
        name="forward",
    )(picked, tiles, empty, *srcs, w_in, w_in_other, w_out, w_out_other, gate)


def back_body(
    feats, dy, oa, ob, ia, ib, act, der, gate, out, dgate,
    dy_v, g_v, o_v, i_v, dh, dy_sem, o_sems, i_sems,
):
    step = pl.program_id(0)
    last = pl.num_programs(0) - 1
    dims = (((1,), (1,)), ((), ()))

    def out_weights(i):
        rows = pl.ds(pl.multiple_of(i * HALF, HALF), HALF)
        slot = i % 2
        return [
            pltpu.make_async_copy(
                w.at[rows, :], o_v.at[slot, pl.ds(k * HALF, HALF), :], o_sems.at[slot, k]
            )
            for k, w in enumerate((oa, ob))
        ]

    def in_weights(i):
        rows = pl.ds(pl.multiple_of(i * feats, feats), feats)
        slot = i % 2
        return [
            pltpu.make_async_copy(
                w.at[rows, pl.ds(j * HALF, HALF)],
                i_v.at[slot, :, pl.ds(j * GROUP + k * HALF, HALF)],
                i_sems.at[slot, k, j],
            )
            for k, w in enumerate((ia, ib))
            for j in range(STEPS)
        ]

    @pl.when(step == 0)
    def _():
        whole = pltpu.make_async_copy(dy, dy_v, dy_sem)
        whole.start()
        start(out_weights(0))
        whole.wait()
        scale = gate[...]
        for f in range(SLICES):
            g = scale * dy_v[f].astype(jnp.float32)
            g_v[:, f * WIDTH : (f + 1) * WIDTH] = g.astype(g_v.dtype)
        dgate[...] = jnp.zeros_like(dgate)

    @pl.when(step < STEPS)
    def _():
        @pl.when(step + 1 < STEPS)
        def _():
            start(out_weights(step + 1))

        @pl.when(step + 1 == STEPS)
        def _():
            start(in_weights(0))

        wait(out_weights(step))
        u = lax.dot_general(g_v[...], o_v[step % 2], dims, preferred_element_type=jnp.float32)
        here = pl.ds(pl.multiple_of(step * GROUP, GROUP), GROUP)
        dh[:, here] = (u * der[...]).astype(dh.dtype)
        total = dgate[...] + jnp.sum(act[...].astype(jnp.float32) * u, axis=1, keepdims=True)
        dgate[...] = jnp.where(step == STEPS - 1, total / gate[...], total)

    @pl.when(step >= STEPS)
    def _():
        i = step - STEPS

        @pl.when(step < last)
        def _():
            start(in_weights(i + 1))

        wait(in_weights(i))
        r = lax.dot_general(dh[...], i_v[i % 2], dims, preferred_element_type=jnp.float32)
        r = r.astype(out.dtype)
        for f in range(out.shape[0]):
            out[f] = r[:, f * WIDTH : (f + 1) * WIDTH]


def back(dy, w_out, w_out_other, w_in, w_in_other, act, der, gate):
    per = 4
    feats = per * WIDTH
    h_spec = pl.BlockSpec((ROWS, GROUP), lambda i: (0, jnp.minimum(i, STEPS - 1)))
    g_spec = pl.BlockSpec((ROWS, 1), lambda i: (0, 0))
    return pl.pallas_call(
        functools.partial(back_body, feats),
        grid=(STEPS + SLICES // per,),
        out_shape=(
            jax.ShapeDtypeStruct((SLICES, ROWS, WIDTH), jnp.bfloat16),
            jax.ShapeDtypeStruct((ROWS, 1), jnp.float32),
        ),
        in_specs=[ANY, ANY, ANY, ANY, ANY, h_spec, h_spec, g_spec],
        out_specs=(
            pl.BlockSpec((per, ROWS, WIDTH), lambda i: (jnp.maximum(i - STEPS, 0), 0, 0)),
            g_spec,
        ),
        scratch_shapes=[
            pltpu.VMEM((SLICES, ROWS, WIDTH), jnp.bfloat16),
            pltpu.VMEM((ROWS, D), jnp.bfloat16),
            pltpu.VMEM((2, GROUP, D), jnp.bfloat16),
            pltpu.VMEM((2, feats, CHIP_UNITS), jnp.bfloat16),
            pltpu.VMEM((ROWS, CHIP_UNITS), jnp.bfloat16),
            pltpu.SemaphoreType.DMA,
            pltpu.SemaphoreType.DMA((2, 2)),
            pltpu.SemaphoreType.DMA((2, 2, STEPS)),
        ],
        compiler_params=params(BACK_MIB),
        cost_estimate=cost(BACK_COST * 4 * ROWS * D * 2 * UNITS, 50 * MIB),
        name="back",
    )(dy, w_out, w_out_other, w_in, w_in_other, act, der, gate)


def merge_body(count, ids, parts, out, total):
    total[...] = jnp.zeros_like(total)

    def step(i, carry):
        total[ids[i]] += parts[i].astype(jnp.float32)
        return carry

    lax.fori_loop(0, count, step, 0)
    out[...] = total[: out.shape[0]].astype(out.dtype)


def merge(parts, ids, blocks):
    count = parts.shape[0]
    return pl.pallas_call(
        functools.partial(merge_body, count),
        out_shape=jax.ShapeDtypeStruct((blocks, BLK, WIDTH), jnp.bfloat16),
        in_specs=[SMEM, VMEM],
        out_specs=VMEM,
        scratch_shapes=[pltpu.VMEM((blocks + 1, BLK, WIDTH), jnp.float32)],
        compiler_params=params(MERGE_MIB),
        cost_estimate=cost(0, (count + blocks) * BLK * WIDTH * 2 * 2),
        name="merge",
    )(ids, parts)


def exchange(value):
    return lax.all_to_all(value, "exp", split_axis=0, concat_axis=0, tiled=True)


def along_z(value, hops, chips):
    pairs = [
        (2 * ((z + hops) % chips) + core, 2 * z + core) for z in range(chips) for core in range(2)
    ]
    return lax.ppermute(value, "tok", pairs)


def other_core(value, chips):
    return lax.ppermute(value, "tok", [(i, i ^ 1) for i in range(2 * chips)])


def on_device(tokens, cotangent, gates, picks, w_in, w_out):
    tile_count = lax.axis_size("tok")
    chips = tile_count // 2
    my_tile = lax.axis_index("tok")
    my_expert = lax.axis_index("exp")
    core = my_tile % 2
    blocks = tokens.shape[0] // BLK
    experts = gates.shape[1]
    w_in, w_out = w_in[0], w_out[0]

    cot_all = lax.all_gather(cotangent.reshape(blocks, BLK, WIDTH), "tok", tiled=True)
    tile_picks = lax.dynamic_index_in_dim(picks, my_tile, 0, False)
    x_slot = pick_blocks(tokens.reshape(blocks, BLK, WIDTH), jnp.minimum(tile_picks, blocks - 1))
    x_mine = exchange(x_slot)

    chosen = picks < blocks
    order = jnp.arange(tile_count, dtype=jnp.int32)
    before = (order[None, :] < order[:, None])[:, :, None] & chosen[None]
    rank = jnp.sum(before.astype(jnp.int32), axis=1)
    slot = jnp.arange(CAP, dtype=jnp.int32)
    at_slot = chosen[:, :, None] & (rank[:, :, None] == slot)
    slot_tile = jnp.sum(jnp.where(at_slot, order[:, None, None], 0), axis=0)
    slot_block = jnp.sum(jnp.where(at_slot, picks[:, :, None], 0), axis=0)
    slot_place = (slot_tile // 2 - my_tile // 2) % chips + chips * ((slot_tile + core) % 2)

    def own_of(values):
        return lax.dynamic_slice_in_dim(values, core * OWN, OWN, 1)

    own_rows = own_of(slot_tile * blocks + slot_block)
    own_places = own_of(slot_place * blocks + slot_block)
    own_tiles = lax.dynamic_index_in_dim(own_of(slot_tile), my_expert, 0, False)
    others = jnp.all(own_tiles[:, None] != order, axis=0)
    at = jnp.sum(((order[:, None] > order) & others).astype(jnp.int32), axis=1)
    free = jnp.arange(tile_count - OWN, dtype=jnp.int32)[:, None]
    empty = jnp.sum(jnp.where(others & (at == free), order, 0), axis=1)
    my_places = lax.dynamic_index_in_dim(own_places, my_expert, 0, False)

    gate_mine = lax.dynamic_index_in_dim(gates, my_expert, 1, False).reshape(blocks, BLK)
    gate_near = jnp.concatenate([gate_mine] + [along_z(gate_mine, k, chips) for k in (1, 2, 3)])
    gate_all = jnp.concatenate([gate_near, other_core(gate_near, chips)])
    gate = jnp.take(gate_all, my_places, axis=0, mode="clip").reshape(ROWS, 1)
    places = my_places // blocks
    x_mine, gate, places, own_tiles, empty = lax.optimization_barrier(
        (x_mine, gate, places, own_tiles, empty)
    )
    above, below = along_z(x_mine, 1, chips), along_z(x_mine, 3, chips)
    far = [along_z(above[:PART], 1, chips), along_z(below[PART:], 3, chips)]
    x_near = [x_mine, above, below, *far]
    send_dy = pick_blocks(cot_all, own_rows.reshape(-1))
    dy = exchange(send_dy.reshape(experts, ROWS, WIDTH))
    x_all = x_near + [other_core(piece, chips) for piece in x_near]
    w_in_other = other_core(w_in, chips)
    w_out_other = other_core(w_out, chips)

    act, der, out_all = forward(
        places, own_tiles, empty, x_all, w_in, w_in_other, w_out, w_out_other, gate, tile_count
    )
    dx_rows, dgate = back(dy, w_out, w_out_other, w_in, w_in_other, act, der, gate)

    out_mine = lax.psum_scatter(out_all, "tok", scatter_dimension=0)
    parts = exchange(dx_rows).reshape(experts * OWN, BLK, WIDTH)
    grad_all = merge(parts, own_rows.reshape(-1), tile_count * blocks)
    d_tokens = lax.psum_scatter(
        grad_all.reshape(tile_count, blocks * BLK, WIDTH), "tok", scatter_dimension=0
    )
    out_mine = exchange(out_mine)
    mixed = merge(out_mine, tile_picks, blocks)

    dgate = dgate.reshape(OWN, BLK)
    dgate += sum(along_z(dgate, k, chips) for k in (1, 2, 3))
    theirs = other_core(dgate, chips)
    low = jnp.where(core == 0, dgate, theirs)
    high = jnp.where(core == 0, theirs, dgate)
    both = jnp.concatenate([low, high])
    both, _ = lax.optimization_barrier((both, out_mine))
    grads = exchange(jnp.broadcast_to(both[None], (experts, CAP, BLK)))
    taken = lax.dynamic_index_in_dim(chosen, my_tile, 0, False)
    here = (slot_tile == my_tile) & taken[:, None]
    mine = jnp.sum(jnp.where(here[:, :, None], grads, 0.0), axis=1)
    at_block = tile_picks[None, :] == jnp.arange(blocks, dtype=jnp.int32)[:, None]
    d_gates = jnp.where(at_block[:, None, :], mine.T[None], 0.0)
    return (
        mixed.reshape(blocks * BLK, WIDTH),
        d_tokens,
        d_gates.reshape(blocks * BLK, experts),
    )


def solution(mesh):
    return jax.shard_map(
        on_device,
        mesh=mesh,
        in_specs=(
            P("tok", "exp"),
            P("tok", "exp"),
            P("tok", None),
            P(),
            P("exp", None, "tok"),
            P("exp", "tok", None),
        ),
        out_specs=(P("tok", "exp"), P("tok", "exp"), P("tok", None)),
        check_vma=False,
    )
```

```python
import functools

import jax
import jax.numpy as jnp
from jax import lax
from jax.experimental import pallas as pl
from jax.experimental.pallas import tpu as pltpu
from jax.sharding import PartitionSpec as P

D = 4096
BLK = 128
WIDTH = 256
SLICES = D // WIDTH
CAP = 6
OWN = CAP // 2
ROWS = OWN * BLK
UNITS = 1024
GELU_C = 0.7978845608028654
GELU_K = 0.044715
MIB = 1024 * 1024
HID_COST = 2
BACK_COST = 16
PICK_MIB, HID_MIB, BACK_MIB, MERGE_MIB = 60, 60, 62, 60
ANY = pl.BlockSpec(memory_space=pl.ANY)
SMEM = pl.BlockSpec(memory_space=pltpu.SMEM)
VMEM = pl.BlockSpec(memory_space=pltpu.VMEM)


def params(mib):
    return pltpu.CompilerParams(vmem_limit_bytes=mib * MIB)


def cost(flops, nbytes):
    return pl.CostEstimate(flops=flops, bytes_accessed=nbytes, transcendentals=0)


def pick_body(count, ids, src, out, sems):
    copies = [
        pltpu.make_async_copy(src.at[ids[i]], out.at[i], sems.at[i]) for i in range(count)
    ]
    for copy in copies:
        copy.start()
    for copy in copies:
        copy.wait()


def pick_blocks(src, ids):
    count = ids.shape[0]
    return pl.pallas_call(
        functools.partial(pick_body, count),
        out_shape=jax.ShapeDtypeStruct((count, BLK, WIDTH), src.dtype),
        in_specs=[SMEM, ANY],
        out_specs=VMEM,
        scratch_shapes=[pltpu.SemaphoreType.DMA((count,))],
        compiler_params=params(PICK_MIB),
        cost_estimate=cost(0, 2 * count * BLK * WIDTH * 2),
        name="pick_blocks",
    )(ids, src)


def as_column(rows):
    shape = (BLK, BLK)
    same = lax.broadcasted_iota(jnp.int32, shape, 0) == lax.broadcasted_iota(jnp.int32, shape, 1)
    parts = [
        jnp.sum(jnp.where(same, rows[s : s + 1, :], 0.0), axis=1, keepdims=True)
        for s in range(OWN)
    ]
    return jnp.concatenate(parts, axis=0)


def start(copies):
    for copy in copies:
        copy.start()


def wait(copies):
    for copy in copies:
        copy.wait()


GROUP = 512
HALF = GROUP // 2
CHIP_UNITS = 2 * UNITS
STEPS = CHIP_UNITS // GROUP
PART = SLICES // 2


def forward_body(sources, feats, picked, tiles, empty, *refs):
    srcs = refs[:sources]
    (
        ia, ib, oa, ob, gate, act, der, out,
        x_raw, x_v, i_v, o_v, act_v, zero_v, r_v, x_sems, i_sems, o_sems, zero_sems, r_sems,
    ) = refs[sources:]
    step = pl.program_id(0)
    last = pl.num_programs(0) - 1
    per = feats // WIDTH

    def in_weights(i):
        cols = pl.ds(pl.multiple_of(i * HALF, HALF), HALF)
        slot = i % 2
        return [
            pltpu.make_async_copy(
                w.at[:, cols], i_v.at[slot, :, pl.ds(k * HALF, HALF)], i_sems.at[slot, k]
            )
            for k, w in enumerate((ia, ib))
        ]

    def out_weights(i):
        cols = pl.ds(pl.multiple_of(i * feats, feats), feats)
        slot = i % 2
        return [
            pltpu.make_async_copy(
                w.at[pl.ds(j * HALF, HALF), cols],
                o_v.at[slot, pl.ds(j * GROUP + k * HALF, HALF), :],
                o_sems.at[slot, k, j],
            )
            for k, w in enumerate((oa, ob))
            for j in range(STEPS)
        ]

    def zeros():
        return [
            pltpu.make_async_copy(zero_v, out.at[empty[k]], zero_sems.at[k])
            for k in range(zero_sems.shape[0])
        ]

    def results(i):
        here = pl.ds(i * per, per)
        return [
            pltpu.make_async_copy(
                r_v.at[i % 2, s], out.at[tiles[s], here], r_sems.at[i % 2, s]
            )
            for s in range(OWN)
        ]

    @pl.when(step == 0)
    def _():
        for s in range(OWN):
            for side in range(2):
                own, above, below, far_a, far_b = srcs[5 * side : 5 * side + 5]
                for hops, source in ((0, own), (1, above), (3, below)):

                    @pl.when(picked[s] == 4 * side + hops)
                    def _(s=s, source=source):
                        pltpu.make_async_copy(source, x_raw.at[s], x_sems.at[s]).start()

                @pl.when(picked[s] == 4 * side + 2)
                def _(s=s, far_a=far_a, far_b=far_b):
                    for source, at in ((far_a, 0), (far_b, PART)):
                        to = x_raw.at[s, pl.ds(at, PART)]
                        pltpu.make_async_copy(source, to, x_sems.at[s]).start()

        start(in_weights(0))
        zero_v[...] = jnp.zeros_like(zero_v)
        for s in range(OWN):
            pltpu.make_async_copy(srcs[0], x_raw.at[s], x_sems.at[s]).wait()
            for f in range(SLICES):
                x_v[s * BLK : (s + 1) * BLK, f * WIDTH : (f + 1) * WIDTH] = x_raw[s, f]

    for k, zero in enumerate(zeros()):

        @pl.when(step == k + 1)
        def _(zero=zero):
            zero.start()

    @pl.when(step < STEPS)
    def _():
        @pl.when(step + 1 < STEPS)
        def _():
            start(in_weights(step + 1))

        @pl.when(step + 1 == STEPS)
        def _():
            start(out_weights(0))

        wait(in_weights(step))
        h = jnp.dot(x_v[...], i_v[step % 2], preferred_element_type=jnp.float32)
        sq = h * h
        t = jnp.tanh(h * (GELU_C + (GELU_C * GELU_K) * sq))
        half = 0.5 + 0.5 * t
        a = (h * half).astype(act.dtype)
        act[...] = a
        act_v[:, pl.ds(pl.multiple_of(step * GROUP, GROUP), GROUP)] = a
        slope = 0.5 * GELU_C + (1.5 * GELU_C * GELU_K) * sq
        der[...] = half + (h * slope) * (1.0 - t * t)

    @pl.when(step >= STEPS)
    def _():
        i = step - STEPS

        @pl.when(step < last)
        def _():
            start(out_weights(i + 1))

        wait(out_weights(i))

        @pl.when(i >= 2)
        def _():
            wait(results(i - 2))

        o = jnp.dot(act_v[...], o_v[i % 2], preferred_element_type=jnp.float32)
        o = (o * as_column(gate[...])).astype(out.dtype)
        for s in range(OWN):
            for f in range(per):
                r_v[i % 2, s, f] = o[s * BLK : (s + 1) * BLK, f * WIDTH : (f + 1) * WIDTH]
        start(results(i))

        @pl.when(step == last)
        def _():
            wait(results(i - 1))
            wait(results(i))
            wait(zeros())


def forward(picked, tiles, empty, srcs, w_in, w_in_other, w_out, w_out_other, gate, tile_count):
    per = 4
    feats = per * WIDTH
    o_spec = pl.BlockSpec((ROWS, GROUP), lambda i: (0, jnp.minimum(i, STEPS - 1)))
    return pl.pallas_call(
        functools.partial(forward_body, len(srcs), feats),
        grid=(STEPS + SLICES // per,),
        out_shape=(
            jax.ShapeDtypeStruct((ROWS, CHIP_UNITS), jnp.bfloat16),
            jax.ShapeDtypeStruct((ROWS, CHIP_UNITS), jnp.float32),
            jax.ShapeDtypeStruct((tile_count, SLICES, BLK, WIDTH), jnp.bfloat16),
        ),
        in_specs=[SMEM] * 3
        + [ANY] * (len(srcs) + 4)
        + [pl.BlockSpec((OWN, BLK), lambda i: (0, 0))],
        out_specs=(o_spec, o_spec, ANY),
        scratch_shapes=[
            pltpu.VMEM((OWN, SLICES, BLK, WIDTH), jnp.bfloat16),
            pltpu.VMEM((ROWS, D), jnp.bfloat16),
            pltpu.VMEM((2, D, GROUP), jnp.bfloat16),
            pltpu.VMEM((2, CHIP_UNITS, feats), jnp.bfloat16),
            pltpu.VMEM((ROWS, CHIP_UNITS), jnp.bfloat16),
            pltpu.VMEM((SLICES, BLK, WIDTH), jnp.bfloat16),
            pltpu.VMEM((2, OWN, per, BLK, WIDTH), jnp.bfloat16),
            pltpu.SemaphoreType.DMA((OWN,)),
            pltpu.SemaphoreType.DMA((2, 2)),
            pltpu.SemaphoreType.DMA((2, 2, STEPS)),
            pltpu.SemaphoreType.DMA((tile_count - OWN,)),
            pltpu.SemaphoreType.DMA((2, OWN)),
        ],
        compiler_params=params(HID_MIB),
        cost_estimate=cost(HID_COST * 2 * ROWS * D * 2 * UNITS, 24 * MIB),
        name="forward",
    )(picked, tiles, empty, *srcs, w_in, w_in_other, w_out, w_out_other, gate)


def back_body(
    feats, dy, oa, ob, ia, ib, act, der, gate, out, dgate,
    dy_v, g_v, o_v, i_v, dh, dy_sem, o_sems, i_sems,
):
    step = pl.program_id(0)
    last = pl.num_programs(0) - 1
    dims = (((1,), (1,)), ((), ()))

    def out_weights(i):
        rows = pl.ds(pl.multiple_of(i * HALF, HALF), HALF)
        slot = i % 2
        return [
            pltpu.make_async_copy(
                w.at[rows, :], o_v.at[slot, pl.ds(k * HALF, HALF), :], o_sems.at[slot, k]
            )
            for k, w in enumerate((oa, ob))
        ]

    def in_weights(i):
        rows = pl.ds(pl.multiple_of(i * feats, feats), feats)
        slot = i % 2
        return [
            pltpu.make_async_copy(
                w.at[rows, pl.ds(j * HALF, HALF)],
                i_v.at[slot, :, pl.ds(j * GROUP + k * HALF, HALF)],
                i_sems.at[slot, k, j],
            )
            for k, w in enumerate((ia, ib))
            for j in range(STEPS)
        ]

    @pl.when(step == 0)
    def _():
        whole = pltpu.make_async_copy(dy, dy_v, dy_sem)
        whole.start()
        start(out_weights(0))
        whole.wait()
        scale = as_column(gate[...])
        for f in range(SLICES):
            g = scale * dy_v[f].astype(jnp.float32)
            g_v[:, f * WIDTH : (f + 1) * WIDTH] = g.astype(g_v.dtype)
        dgate[...] = jnp.zeros_like(dgate)

    @pl.when(step < STEPS)
    def _():
        @pl.when(step + 1 < STEPS)
        def _():
            start(out_weights(step + 1))

        @pl.when(step + 1 == STEPS)
        def _():
            start(in_weights(0))

        wait(out_weights(step))
        u = lax.dot_general(g_v[...], o_v[step % 2], dims, preferred_element_type=jnp.float32)
        here = pl.ds(pl.multiple_of(step * GROUP, GROUP), GROUP)
        dh[:, here] = (u * der[...]).astype(dh.dtype)
        total = dgate[...] + jnp.sum(act[...].astype(jnp.float32) * u, axis=1, keepdims=True)
        dgate[...] = jnp.where(step == STEPS - 1, total / as_column(gate[...]), total)

    @pl.when(step >= STEPS)
    def _():
        i = step - STEPS

        @pl.when(step < last)
        def _():
            start(in_weights(i + 1))

        wait(in_weights(i))
        r = lax.dot_general(dh[...], i_v[i % 2], dims, preferred_element_type=jnp.float32)
        r = r.astype(out.dtype)
        for f in range(out.shape[0]):
            out[f] = r[:, f * WIDTH : (f + 1) * WIDTH]


def back(dy, w_out, w_out_other, w_in, w_in_other, act, der, gate):
    per = 4
    feats = per * WIDTH
    h_spec = pl.BlockSpec((ROWS, GROUP), lambda i: (0, jnp.minimum(i, STEPS - 1)))
    g_spec = pl.BlockSpec((ROWS, 1), lambda i: (0, 0))
    return pl.pallas_call(
        functools.partial(back_body, feats),
        grid=(STEPS + SLICES // per,),
        out_shape=(
            jax.ShapeDtypeStruct((SLICES, ROWS, WIDTH), jnp.bfloat16),
            jax.ShapeDtypeStruct((ROWS, 1), jnp.float32),
        ),
        in_specs=[ANY] * 5 + [h_spec, h_spec, pl.BlockSpec((OWN, BLK), lambda i: (0, 0))],
        out_specs=(
            pl.BlockSpec((per, ROWS, WIDTH), lambda i: (jnp.maximum(i - STEPS, 0), 0, 0)),
            g_spec,
        ),
        scratch_shapes=[
            pltpu.VMEM((SLICES, ROWS, WIDTH), jnp.bfloat16),
            pltpu.VMEM((ROWS, D), jnp.bfloat16),
            pltpu.VMEM((2, GROUP, D), jnp.bfloat16),
            pltpu.VMEM((2, feats, CHIP_UNITS), jnp.bfloat16),
            pltpu.VMEM((ROWS, CHIP_UNITS), jnp.bfloat16),
            pltpu.SemaphoreType.DMA,
            pltpu.SemaphoreType.DMA((2, 2)),
            pltpu.SemaphoreType.DMA((2, 2, STEPS)),
        ],
        compiler_params=params(BACK_MIB),
        cost_estimate=cost(BACK_COST * 4 * ROWS * D * 2 * UNITS, 50 * MIB),
        name="back",
    )(dy, w_out, w_out_other, w_in, w_in_other, act, der, gate)


def merge_body(count, ids, parts, out, total):
    total[...] = jnp.zeros_like(total)

    def step(i, carry):
        total[ids[i]] += parts[i].astype(jnp.float32)
        return carry

    lax.fori_loop(0, count, step, 0)
    out[...] = total[: out.shape[0]].astype(out.dtype)


def merge(parts, ids, blocks):
    count = parts.shape[0]
    return pl.pallas_call(
        functools.partial(merge_body, count),
        out_shape=jax.ShapeDtypeStruct((blocks, BLK, WIDTH), jnp.bfloat16),
        in_specs=[SMEM, VMEM],
        out_specs=VMEM,
        scratch_shapes=[pltpu.VMEM((blocks + 1, BLK, WIDTH), jnp.float32)],
        compiler_params=params(MERGE_MIB),
        cost_estimate=cost(0, (count + blocks) * BLK * WIDTH * 2 * 2),
        name="merge",
    )(ids, parts)


def exchange(value):
    return lax.all_to_all(value, "exp", split_axis=0, concat_axis=0, tiled=True)


def along_z(value, hops, chips):
    pairs = [
        (2 * ((z + hops) % chips) + core, 2 * z + core) for z in range(chips) for core in range(2)
    ]
    return lax.ppermute(value, "tok", pairs)


def other_core(value, chips):
    return lax.ppermute(value, "tok", [(i, i ^ 1) for i in range(2 * chips)])


def on_device(tokens, cotangent, gates, picks, w_in, w_out):
    tile_count = lax.axis_size("tok")
    chips = tile_count // 2
    my_tile = lax.axis_index("tok")
    my_expert = lax.axis_index("exp")
    core = my_tile % 2
    blocks = tokens.shape[0] // BLK
    experts = gates.shape[1]
    w_in, w_out = w_in[0], w_out[0]

    cot_all = lax.all_gather(cotangent.reshape(blocks, BLK, WIDTH), "tok", tiled=True)
    tile_picks = lax.dynamic_index_in_dim(picks, my_tile, 0, False)
    x_slot = pick_blocks(tokens.reshape(blocks, BLK, WIDTH), jnp.minimum(tile_picks, blocks - 1))
    x_mine = exchange(x_slot)

    chosen = picks < blocks
    order = jnp.arange(tile_count, dtype=jnp.int32)
    before = (order[None, :] < order[:, None])[:, :, None] & chosen[None]
    rank = jnp.sum(before.astype(jnp.int32), axis=1)
    slot = jnp.arange(CAP, dtype=jnp.int32)
    at_slot = chosen[:, :, None] & (rank[:, :, None] == slot)
    slot_tile = jnp.sum(jnp.where(at_slot, order[:, None, None], 0), axis=0)
    slot_block = jnp.sum(jnp.where(at_slot, picks[:, :, None], 0), axis=0)
    slot_place = (slot_tile // 2 - my_tile // 2) % chips + chips * ((slot_tile + core) % 2)

    def own_of(values):
        return lax.dynamic_slice_in_dim(values, core * OWN, OWN, 1)

    own_rows = own_of(slot_tile * blocks + slot_block)
    own_places = own_of(slot_place * blocks + slot_block)
    own_tiles = lax.dynamic_index_in_dim(own_of(slot_tile), my_expert, 0, False)
    others = jnp.all(own_tiles[:, None] != order, axis=0)
    at = jnp.sum(((order[:, None] > order) & others).astype(jnp.int32), axis=1)
    free = jnp.arange(tile_count - OWN, dtype=jnp.int32)[:, None]
    empty = jnp.sum(jnp.where(others & (at == free), order, 0), axis=1)
    my_places = lax.dynamic_index_in_dim(own_places, my_expert, 0, False)

    gate_mine = lax.dynamic_index_in_dim(gates, my_expert, 1, False).reshape(blocks, BLK)
    gate_mine, _ = lax.optimization_barrier((gate_mine, x_slot))
    gate_near = jnp.concatenate([gate_mine] + [along_z(gate_mine, k, chips) for k in (1, 2, 3)])
    gate_all = jnp.concatenate([gate_near, other_core(gate_near, chips)])
    gate = jnp.take(gate_all, my_places, axis=0, mode="clip")
    places = my_places // blocks
    w_in_other = other_core(w_in, chips)
    w_out_other = other_core(w_out, chips)
    x_mine, gate, places, own_tiles, empty, w_in_other, w_out_other = lax.optimization_barrier(
        (x_mine, gate, places, own_tiles, empty, w_in_other, w_out_other)
    )
    above, below = along_z(x_mine, 1, chips), along_z(x_mine, 3, chips)
    far = [along_z(above[:PART], 1, chips), along_z(below[PART:], 3, chips)]
    x_near = [x_mine, above, below, *far]
    send_dy = pick_blocks(cot_all, own_rows.reshape(-1))
    dy = exchange(send_dy.reshape(experts, ROWS, WIDTH))
    x_all = x_near + [other_core(piece, chips) for piece in x_near]

    act, der, out_all = forward(
        places, own_tiles, empty, x_all, w_in, w_in_other, w_out, w_out_other, gate, tile_count
    )
    dx_rows, dgate = back(dy, w_out, w_out_other, w_in, w_in_other, act, der, gate)

    out_mine = lax.psum_scatter(out_all, "tok", scatter_dimension=0)
    parts = exchange(dx_rows).reshape(experts * OWN, BLK, WIDTH)
    grad_all = merge(parts, own_rows.reshape(-1), tile_count * blocks)
    d_tokens = lax.psum_scatter(
        grad_all.reshape(tile_count, blocks * BLK, WIDTH), "tok", scatter_dimension=0
    )
    out_mine = exchange(out_mine)
    mixed = merge(out_mine, tile_picks, blocks)

    dgate = dgate.reshape(OWN, BLK)
    dgate += sum(along_z(dgate, k, chips) for k in (1, 2, 3))
    theirs = other_core(dgate, chips)
    low = jnp.where(core == 0, dgate, theirs)
    high = jnp.where(core == 0, theirs, dgate)
    both = jnp.concatenate([low, high])
    both, _ = lax.optimization_barrier((both, out_mine))
    grads = exchange(jnp.broadcast_to(both[None], (experts, CAP, BLK)))
    taken = lax.dynamic_index_in_dim(chosen, my_tile, 0, False)
    here = (slot_tile == my_tile) & taken[:, None]
    mine = jnp.sum(jnp.where(here[:, :, None], grads, 0.0), axis=1)
    at_block = tile_picks[None, :] == jnp.arange(blocks, dtype=jnp.int32)[:, None]
    d_gates = jnp.where(at_block[:, None, :], mine.T[None], 0.0)
    return (
        mixed.reshape(blocks * BLK, WIDTH),
        d_tokens,
        d_gates.reshape(blocks * BLK, experts),
    )


def solution(mesh):
    return jax.shard_map(
        on_device,
        mesh=mesh,
        in_specs=(
            P("tok", "exp"),
            P("tok", "exp"),
            P("tok", None),
            P(),
            P("exp", None, "tok"),
            P("exp", "tok", None),
        ),
        out_specs=(P("tok", "exp"), P("tok", "exp"), P("tok", None)),
        check_vma=False,
    )
```
